512 devices in a mesh: dp: 16 (over z), fsdp: 32 (over y, x, core).
Axes of the slice: x: 4, y: 4, z: 16, core: 2. Of those that a mesh axis runs over, the one named last changes fastest.
Arguments:
- features: bfloat16 [32768, 8192], P('dp', 'fsdp'), may hold values from -6 to 6
- out_cotangent: bfloat16 [32768, 8192], P('dp', 'fsdp'), may hold values from -0.3125 to 0.3125
- head_cotangents: bfloat16 [32768, 1280], P(('dp', 'fsdp')), may hold values from -0.3125 to 0.3125
- attention_out: bfloat16 [32768, 1024], P(('dp', 'fsdp')), may hold values from -6 to 6
- momentum: float32 [18, 8192, 128], P(None, 'fsdp'), may hold values from -6 to 6
- lengths: int32 [16], P('dp'), may hold values from 1 to 2048
Outputs:
- updates: bfloat16 [18, 8192, 128], P(None, 'fsdp')
The draws below stay inside these ranges and needn't reach their ends.
All inputs are finite; a program needn't handle non-finite values.
Results may differ from the reference program's by a relative error of at most 0.0052.
Values may be sent and summed in bfloat16 or wider, within the bound.
No kernel may reach another device: no remote copies, remote signals or barrier semaphores. Data moves between devices by JAX's collectives and lax.ppermute only.
A program may use at most 64 MiB of HBM per device.

```python
import math
import jax
import jax.numpy as jnp
from jax import lax

D = 8192
HEAD = 128
KV_WIN = 1
ITERS = 3
SLOT = 2048
QH = 8
MATS = 18
TOKENS = 32768
NSEQ = 16


def set_ends(entries, key, least, largest):
    extent = entries.shape
    index_at = [jax.random.randint(jax.random.fold_in(key, axis), (), 0, extent[axis]) for axis in range(len(extent))]
    entries = entries.at[tuple(index_at)].set(least)
    longest = extent.index(max(extent))
    index_at[longest] = (index_at[longest] + 1) % extent[longest]
    return entries.at[tuple(index_at)].set(largest)


def block_levels(rng, extent, cuts, low, high):
    factor_of = 1.0
    for axis_at, blocks in cuts:
        heights = jax.random.uniform(jax.random.fold_in(jax.random.fold_in(rng, 6), axis_at), (blocks,), jnp.float32, low / len(cuts), high / len(cuts))
        factor_of = factor_of * jnp.repeat(jnp.exp(heights), extent[axis_at] // blocks).reshape((-1,) + (1,) * (len(extent) - 1 - axis_at))
    return factor_of


def scatter_about(rng, shape, deviation, bound, split=(), kind=jnp.bfloat16):
    result = deviation * jax.random.normal(rng, shape, jnp.float32)
    if split:
        result = result * block_levels(rng, shape, split, -0.22, 0.18)
    return jnp.clip(result, -bound, bound).astype(kind)


def setup_inputs(seed: int = 0) -> dict:
    key_list = jax.random.split(jax.random.key(seed), 7)
    return {
        "features": scatter_about(key_list[0], (TOKENS, D), 1.0, 6.0, ((0, 16), (1, 32))),
        "out_cotangent": scatter_about(key_list[1], (TOKENS, D), 0.02, 0.3125, ((0, 16), (1, 32))),
        "head_cotangents": scatter_about(key_list[2], (TOKENS, (QH + 2 * KV_WIN) * HEAD), 0.02, 0.3125, ((0, 512),)),
        "attention_out": scatter_about(key_list[3], (TOKENS, QH * HEAD), 1.0, 6.0, ((0, 512),)),
        "momentum": scatter_about(key_list[4], (MATS, D, HEAD), 1.0, 6.0, ((1, 32),), jnp.float32),
        "lengths": set_ends(jax.random.randint(key_list[5], (NSEQ,), 1, SLOT + 1), jax.random.fold_in(key_list[5], 1), 1, SLOT).astype(jnp.int32),
    }


coef_a = 3.4445
coef_b = -4.775
coef_c = 2.0315
momentum_decay = 0.95
update_gain = 0.2
norm_floor = 1e-07

def orthogonal_part(blended):
    highest = lax.Precision.HIGHEST
    sum_squares = lax.optimization_barrier(jnp.sum(blended * blended, axis=(1, 2)))
    iterate = blended / (jnp.sqrt(sum_squares) + norm_floor)[:, None, None]
    for iteration in range(ITERS):
        gram_sum = jnp.einsum('mrc,mrd->mcd', iterate, iterate, precision=highest)
        poly_term = coef_b * gram_sum + coef_c * jnp.einsum('mcd,mde->mce', gram_sum, gram_sum, precision=highest)
        iterate = coef_a * iterate + jnp.einsum('mrc,mcd->mrd', iterate, poly_term, precision=highest)
    return iterate

def reference(features, out_cotangent, head_cotangents, attention_out, momentum, lengths):
    positions = jnp.arange(TOKENS, dtype=jnp.int32)
    limits = lengths[positions // SLOT]
    live_mask = (positions % SLOT < limits).astype(jnp.bfloat16)[:, None]
    grad_in = jnp.dot((features * live_mask).T, head_cotangents, preferred_element_type=jnp.float32)
    grad_out = jnp.dot((out_cotangent * live_mask).T, attention_out, preferred_element_type=jnp.float32)
    gradient = jnp.concatenate([grad_in, grad_out], axis=1).reshape(D, MATS, HEAD).transpose(1, 0, 2)
    new_moment = momentum_decay * momentum + gradient
    blended = (gradient + momentum_decay * new_moment).astype(jnp.bfloat16)
    blended = lax.optimization_barrier(blended).astype(jnp.float32)
    iterate = orthogonal_part(blended)
    return (update_gain * math.sqrt(max(D, HEAD)) * iterate).astype(jnp.bfloat16)
```

```python
import math

import jax
import jax.numpy as jnp
from jax import lax
from jax.sharding import PartitionSpec as P

ITERS = 3


coef_a = 3.4445
coef_b = -4.775
coef_c = 2.0315
momentum_decay = 0.95
update_gain = 0.2
norm_floor = 1e-07


def nesterov_blend(gradient, moment_rows):
    new_moment = momentum_decay * moment_rows + gradient
    return (gradient + momentum_decay * new_moment).astype(jnp.bfloat16)


def poly_of_gram(gram, out_scale):
    highest = lax.Precision.HIGHEST

    def mul(left, right):
        return jnp.einsum("mij,mjk->mik", left, right, precision=highest)

    size = gram.shape[-1]
    eye = jnp.eye(size, dtype=jnp.float32)[None]
    sum_squares = jnp.sum(gram * eye, axis=(1, 2), keepdims=True)
    inverse = 1.0 / (jnp.sqrt(sum_squares) + norm_floor)
    current = gram * inverse * inverse
    factor = eye * (inverse * out_scale)
    for iteration in range(ITERS):
        step = coef_a * eye + coef_b * current + coef_c * mul(current, current)
        factor = mul(factor, step) if iteration else factor[:, :1, :1] * step
        if iteration < ITERS - 1:
            current = mul(mul(current, step), step)
    return factor


def split_product(rows, factor):
    high = factor.astype(jnp.bfloat16)
    low = (factor - high.astype(jnp.float32)).astype(jnp.bfloat16)
    product = jnp.dot(rows, high, preferred_element_type=jnp.float32)
    product += jnp.dot(rows, low, preferred_element_type=jnp.float32)
    return product.astype(jnp.bfloat16)


def local(features, out_cotangent, head_cotangents, attention_out, momentum, lengths):
    tok_count, row_count = features.shape
    mat_count, _, head_size = momentum.shape
    groups, owners = lax.axis_size("dp"), lax.axis_size("fsdp")
    in_width = head_cotangents.shape[1]
    group = lax.axis_index("dp")
    extra = mat_count - groups
    share = extra * row_count // groups
    per_extra = groups // extra

    live = lax.iota(jnp.int32, tok_count) < lengths[0]
    live_mask = live.astype(jnp.bfloat16)[:, None]
    heads = lax.all_gather(
        jnp.concatenate([head_cotangents, attention_out], axis=1), "fsdp", axis=0, tiled=True
    )
    contract = (((0,), (0,)), ((), ()))
    part_in = lax.dot_general(
        features * live_mask, heads[:, :in_width], contract, preferred_element_type=jnp.float32
    )
    part_out = lax.dot_general(
        out_cotangent * live_mask, heads[:, in_width:], contract, preferred_element_type=jnp.float32
    )
    partial = jnp.concatenate([part_in, part_out], axis=1).astype(jnp.bfloat16)
    partial = partial.reshape(row_count, mat_count, head_size).transpose(1, 0, 2)
    partial = jnp.concatenate(
        [partial[:groups], partial[groups:].reshape(groups, share, head_size)], axis=1
    )
    received = lax.all_to_all(partial, "dp", 0, 0, tiled=True)
    gradient = jnp.sum(received.astype(jnp.float32), axis=0)
    moment_main = lax.dynamic_index_in_dim(momentum, group, 0, keepdims=False)
    moment_rest = lax.dynamic_index_in_dim(
        momentum[groups:].reshape(groups, share, head_size), group, 0, keepdims=False
    )
    main = nesterov_blend(gradient[:row_count], moment_main)
    rest = nesterov_blend(gradient[row_count:], moment_rest)

    gram_main = lax.dot_general(main, main, contract, preferred_element_type=jnp.float32)
    gram_rest = lax.dot_general(rest, rest, contract, preferred_element_type=jnp.float32)
    slab = head_size // owners
    both = jnp.concatenate(
        [gram_main.reshape(owners, slab, head_size), gram_rest.reshape(owners, slab, head_size)], axis=1
    )
    summed = jnp.sum(lax.all_to_all(both, "fsdp", 0, 0, tiled=True), axis=0)
    octets = [[e * per_extra + i for i in range(per_extra)] for e in range(extra)]
    rest_sum = jnp.sum(
        lax.all_to_all(
            jnp.broadcast_to(summed[None, slab:], (per_extra, slab, head_size)),
            "dp", 0, 0, axis_index_groups=octets, tiled=True,
        ),
        axis=0,
    )
    summed = jnp.concatenate([summed[:slab], rest_sum], axis=0)
    grams = lax.all_to_all(
        jnp.broadcast_to(summed[None], (owners, 2 * slab, head_size)), "fsdp", 0, 0, tiled=True
    )
    grams = grams.reshape(owners, 2, slab, head_size).transpose(1, 0, 2, 3)
    out_scale = update_gain * math.sqrt(max(row_count * owners, head_size))
    factors = poly_of_gram(grams.reshape(2, head_size, head_size), out_scale)
    update_main = split_product(main, factors[0])
    update_rest = split_product(rest, factors[1])

    cut = row_count - share
    first = lax.all_gather(update_main[:cut], "dp", axis=0)
    tail = jnp.concatenate([update_main[cut:], update_rest], axis=0)
    second = lax.all_to_all(
        jnp.broadcast_to(tail[None], (groups,) + tail.shape), "dp", 0, 0, tiled=True
    )
    mains = jnp.concatenate([first, second[:, :share]], axis=1)
    rests = second[:, share:].reshape(extra, row_count, head_size)
    return jnp.concatenate([mains, rests], axis=0)


def solution(mesh):
    return jax.shard_map(
        local,
        mesh=mesh,
        in_specs=(
            P("dp", "fsdp"),
            P("dp", "fsdp"),
            P(("dp", "fsdp"), None),
            P(("dp", "fsdp"), None),
            P(None, "fsdp", None),
            P("dp"),
        ),
        out_specs=P(None, "fsdp", None),
        check_vma=False,
    )
```

```python
import math

import jax
import jax.numpy as jnp
from jax import lax
from jax.sharding import PartitionSpec as P

ITERS = 3
EARLY = 32


coef_a = 3.4445
coef_b = -4.775
coef_c = 2.0315
momentum_decay = 0.95
update_gain = 0.2
norm_floor = 1e-07


def nesterov_blend(gradient, moment_rows):
    new_moment = momentum_decay * moment_rows + gradient
    return (gradient + momentum_decay * new_moment).astype(jnp.bfloat16)


def poly_of_gram(gram, out_scale):
    highest = lax.Precision.HIGHEST

    def mul(left, right):
        return jnp.einsum("mij,mjk->mik", left, right, precision=highest)

    size = gram.shape[-1]
    eye = jnp.eye(size, dtype=jnp.float32)[None]
    sum_squares = jnp.sum(gram * eye, axis=(1, 2), keepdims=True)
    inverse = 1.0 / (jnp.sqrt(sum_squares) + norm_floor)
    current = gram * inverse * inverse
    factor = eye * (inverse * out_scale)
    for iteration in range(ITERS):
        step = coef_a * eye + coef_b * current + coef_c * mul(current, current)
        factor = mul(factor, step) if iteration else factor[:, :1, :1] * step
        if iteration < ITERS - 1:
            current = mul(mul(current, step), step)
    return factor


def split_product(columns, factor):
    high = lax.reduce_precision(factor, 8, 7)
    contract = (((0,), (0,)), ((), ()))
    parts = [
        lax.dot_general(columns, part.astype(jnp.bfloat16), contract, preferred_element_type=jnp.float32)
        for part in (high, factor - high)
    ]
    return (parts[0] + parts[1]).astype(jnp.bfloat16)


def local(features, out_cotangent, head_cotangents, attention_out, momentum, lengths):
    tok_count, row_count = features.shape
    mat_count, _, head_size = momentum.shape
    groups, owners = lax.axis_size("dp"), lax.axis_size("fsdp")
    own_tok = head_cotangents.shape[0]
    in_mats = head_cotangents.shape[1] // head_size
    out_mats = groups - in_mats
    extra = mat_count - groups
    share = extra * head_size // groups
    cores = 2
    places = owners // cores
    group, core = lax.axis_index("dp"), lax.axis_index("fsdp") % cores
    same_core = [list(range(c, owners, cores)) for c in range(cores)]
    across = [(i, i ^ 1) for i in range(owners)]

    head3 = head_cotangents.reshape(own_tok, in_mats, head_size)
    attn3 = attention_out.reshape(own_tok, mat_count - in_mats, head_size)

    def pick(low, high):
        return [
            head3[:, :, low:high].reshape(own_tok, in_mats * (high - low)),
            attn3[:, :out_mats, low:high].reshape(own_tok, out_mats * (high - low)),
        ]

    late_heads = lax.all_gather(
        jnp.concatenate(pick(EARLY, head_size), axis=1), "fsdp", axis=0, tiled=True
    )
    early_own = jnp.concatenate(
        pick(0, EARLY) + [attn3[:, out_mats:].reshape(own_tok, extra * head_size)], axis=1
    )
    mine = lax.all_to_all(
        jnp.broadcast_to(early_own[None], (places,) + early_own.shape),
        "fsdp", 0, 0, axis_index_groups=same_core, tiled=True,
    ).reshape(places * own_tok, early_own.shape[1])
    other = lax.ppermute(mine, "fsdp", across)

    live_mask = (lax.iota(jnp.int32, tok_count) < lengths[0]).astype(jnp.bfloat16)[:, None]

    def halves(rows):
        split = (rows * live_mask).reshape(places, cores, own_tok, row_count)
        return [
            lax.dynamic_index_in_dim(split, which, 1, keepdims=False).reshape(-1, row_count)
            for which in (core, 1 - core)
        ]

    def product(heads, rows):
        contract = (((0,), (0,)), ((), ()))
        return lax.dot_general(heads, rows, contract, preferred_element_type=jnp.float32)

    feature_halves, cotangent_halves = halves(features), halves(out_cotangent)
    cut = in_mats * EARLY
    early_in = product(mine[:, :cut], feature_halves[0]) + product(other[:, :cut], feature_halves[1])
    early_out = product(mine[:, cut:], cotangent_halves[0]) + product(other[:, cut:], cotangent_halves[1])
    early = jnp.concatenate([early_in, early_out], axis=0).astype(jnp.bfloat16)
    early = jnp.concatenate(
        [
            early[: groups * EARLY].reshape(groups, EARLY, row_count),
            early[groups * EARLY :].reshape(groups, share, row_count),
        ],
        axis=1,
    )
    early = lax.all_to_all(early, "dp", 0, 0, tiled=True)

    cut = in_mats * (head_size - EARLY)
    late_in = product(late_heads[:, :cut], features * live_mask)
    late_out = product(late_heads[:, cut:], out_cotangent * live_mask)
    late = jnp.concatenate([late_in, late_out], axis=0).astype(jnp.bfloat16)
    early, late = lax.optimization_barrier((early, late))
    early_sum = jnp.sum(early.astype(jnp.float32), axis=0)

    moment_main = lax.dynamic_index_in_dim(momentum, group, 0, keepdims=False).T
    moment_rest = lax.dynamic_index_in_dim(
        momentum[groups:].transpose(0, 2, 1).reshape(groups, share, row_count), group, 0, keepdims=False
    )
    rest = nesterov_blend(early_sum[EARLY:], moment_rest)

    late = late.reshape(groups, head_size - EARLY, row_count)
    late = jnp.concatenate([late, jnp.broadcast_to(rest[None], (groups, share, row_count))], axis=1)
    late = lax.all_to_all(late, "dp", 0, 0, tiled=True)
    late_sum = jnp.sum(late[:, : head_size - EARLY].astype(jnp.float32), axis=0)
    rest = late[:, head_size - EARLY :].reshape(extra, head_size, row_count)
    main = jnp.concatenate(
        [
            nesterov_blend(early_sum[:EARLY], moment_main[:EARLY]),
            nesterov_blend(late_sum, moment_main[EARLY:]),
        ],
        axis=0,
    )

    def gram(columns):
        return lax.dot_general(columns, columns, (((1,), (1,)), ((), ())), preferred_element_type=jnp.float32)

    slab = head_size // owners
    blended = [main] + [rest[e] for e in range(extra)]
    grams = jnp.stack([gram(b).reshape(owners, slab, head_size) for b in blended], axis=1)
    grams = grams.reshape(owners, (1 + extra) * slab, head_size)
    summed = jnp.sum(lax.all_to_all(grams, "fsdp", 0, 0, tiled=True), axis=0)
    grams = lax.all_to_all(jnp.broadcast_to(summed[None], grams.shape), "fsdp", 0, 0, tiled=True)
    grams = grams.reshape(owners, 1 + extra, slab, head_size).transpose(1, 0, 2, 3)
    out_scale = update_gain * math.sqrt(max(row_count * owners, head_size))
    factors = poly_of_gram(grams.reshape(1 + extra, head_size, head_size), out_scale)
    update = split_product(main, factors[0])
    cut = row_count - row_count // groups
    tail = jnp.broadcast_to(update[None, cut:], (groups, row_count - cut, head_size))
    tails = lax.all_to_all(tail, "dp", 0, 0, tiled=True)
    updates = lax.all_gather(update[:cut], "dp", axis=0)
    rests = jnp.stack([split_product(rest[e], factors[1 + e]) for e in range(extra)])
    return jnp.concatenate([jnp.concatenate([updates, tails], axis=1), rests], axis=0)


def solution(mesh):
    return jax.shard_map(
        local,
        mesh=mesh,
        in_specs=(
            P("dp", "fsdp"),
            P("dp", "fsdp"),
            P(("dp", "fsdp"), None),
            P(("dp", "fsdp"), None),
            P(None, "fsdp", None),
            P("dp"),
        ),
        out_specs=P(None, "fsdp", None),
        check_vma=False,
    )
```

```python
import math

import jax
import jax.numpy as jnp
from jax import lax
from jax.sharding import Mesh
from jax.sharding import PartitionSpec as P

ITERS = 3
EARLY = 32


coef_a = 3.4445
coef_b = -4.775
coef_c = 2.0315
momentum_decay = 0.95
update_gain = 0.2
norm_floor = 1e-07


def nesterov_blend(gradient, moment_rows):
    new_moment = momentum_decay * moment_rows + gradient
    return (gradient + momentum_decay * new_moment).astype(jnp.bfloat16)


def poly_of_gram(gram, out_scale):
    highest = lax.Precision.HIGHEST

    def mul(left, right):
        return jnp.einsum("mij,mjk->mik", left, right, precision=highest)

    size = gram.shape[-1]
    eye = jnp.eye(size, dtype=jnp.float32)[None]
    sum_squares = jnp.sum(gram * eye, axis=(1, 2), keepdims=True)
    inverse = 1.0 / (jnp.sqrt(sum_squares) + norm_floor)
    current = gram * inverse * inverse
    factor = eye * (inverse * out_scale)
    for iteration in range(ITERS):
        step = coef_a * eye + coef_b * current + coef_c * mul(current, current)
        factor = mul(factor, step) if iteration else factor[:, :1, :1] * step
        if iteration < ITERS - 1:
            current = mul(mul(current, step), step)
    return factor


def split_product(columns, factor):
    high = lax.reduce_precision(factor, 8, 7)
    contract = (((0,), (0,)), ((), ()))
    parts = [
        lax.dot_general(columns, part.astype(jnp.bfloat16), contract, preferred_element_type=jnp.float32)
        for part in (high, factor - high)
    ]
    return (parts[0] + parts[1]).astype(jnp.bfloat16)


def local(features, out_cotangent, head_cotangents, attention_out, momentum, lengths):
    tok_count, row_count = features.shape
    mat_count, _, head_size = momentum.shape
    own_tok = head_cotangents.shape[0]
    pairs, places = lax.axis_size("pair"), lax.axis_size("place")
    cores = lax.axis_size("core")
    groups, owners = 2 * pairs, places * cores
    in_mats = head_cotangents.shape[1] // head_size
    share = head_size // pairs
    late_width = head_size - EARLY
    pair, side, core = lax.axis_index("pair"), lax.axis_index("side"), lax.axis_index("core")

    def exchange(array, axis):
        return lax.ppermute(array, axis, [(0, 1), (1, 0)])

    def product(heads, rows):
        contract = (((0,), (0,)), ((), ()))
        return lax.dot_general(heads, rows, contract, preferred_element_type=jnp.float32)

    heads = jnp.concatenate([head_cotangents, attention_out], axis=1).reshape(own_tok, mat_count, head_size)
    late_heads = lax.all_gather(
        heads[:, :groups, EARLY:].reshape(own_tok, groups * late_width), ("place", "core"), axis=0, tiled=True
    )

    early_own = jnp.concatenate(
        [
            heads[:, :groups, :EARLY].reshape(own_tok, groups * EARLY),
            heads[:, groups:].reshape(own_tok, (mat_count - groups) * head_size),
        ],
        axis=1,
    )
    mine = lax.all_to_all(
        jnp.broadcast_to(early_own[None], (places,) + early_own.shape), "place", 0, 0, tiled=True
    ).reshape(places * own_tok, early_own.shape[1])
    live_mask = (lax.iota(jnp.int32, tok_count) < lengths[0]).astype(jnp.bfloat16)[:, None]
    rows_in, rows_out = features * live_mask, out_cotangent * live_mask

    def halves(rows):
        split = rows.reshape(places, cores, own_tok, row_count)
        return [
            lax.dynamic_index_in_dim(split, which, 1, keepdims=False).reshape(-1, row_count)
            for which in (core, 1 - core)
        ]

    halves_in, halves_out = halves(rows_in), halves(rows_out)
    mine, halves_in, halves_out = lax.optimization_barrier((mine, halves_in, halves_out))
    other = exchange(mine, "core")
    cut = in_mats * EARLY
    early_in = product(mine[:, :cut], halves_in[0]) + product(other[:, :cut], halves_in[1])
    early_out = product(mine[:, cut:], halves_out[0]) + product(other[:, cut:], halves_out[1])
    early = jnp.concatenate([early_in, early_out], axis=0).astype(jnp.bfloat16)
    rest = early[groups * EARLY :].reshape(2, pairs, share, row_count).transpose(1, 0, 2, 3)
    early = jnp.concatenate(
        [early[: groups * EARLY].reshape(groups, EARLY, row_count), rest.reshape(groups, share, row_count)], axis=1
    )
    early = lax.all_to_all(early, ("pair", "side"), 0, 0, tiled=True)

    cut = in_mats * late_width
    late = jnp.concatenate(
        [
            product(late_heads[:, :cut], features * live_mask),
            product(late_heads[:, cut:], out_cotangent * live_mask),
        ],
        axis=0,
    ).reshape(pairs, 2, late_width, row_count)
    keep = jnp.where(side == 0, late[:, 0], late[:, 1])
    give = jnp.where(side == 0, late[:, 1], late[:, 0]).astype(jnp.bfloat16)
    early, keep, give = lax.optimization_barrier((early, keep, give))
    got = exchange(give, "side")
    late = (keep + got.astype(jnp.float32)).astype(jnp.bfloat16)
    early_sum = jnp.sum(early.astype(jnp.float32), axis=0)

    moment_main = lax.dynamic_index_in_dim(momentum, 2 * pair + side, 0, keepdims=False).T
    moment_rest = lax.dynamic_index_in_dim(momentum, groups + side, 0, keepdims=False).T
    moment_rest = lax.dynamic_slice_in_dim(moment_rest, pair * share, share, axis=0)
    rest = nesterov_blend(early_sum[EARLY:], moment_rest)

    late = jnp.concatenate([late, jnp.broadcast_to(rest[None], (pairs, share, row_count))], axis=1)
    late = lax.all_to_all(late, "pair", 0, 0, tiled=True)
    late_sum = jnp.sum(late[:, :late_width].astype(jnp.float32), axis=0)
    rest = late[:, late_width:].reshape(head_size, row_count)
    main = jnp.concatenate(
        [
            nesterov_blend(early_sum[:EARLY], moment_main[:EARLY]),
            nesterov_blend(late_sum, moment_main[EARLY:]),
        ],
        axis=0,
    )

    def gram(columns):
        return lax.dot_general(columns, columns, (((1,), (1,)), ((), ())), preferred_element_type=jnp.float32)

    slab = head_size // owners
    grams = jnp.concatenate([gram(b).reshape(owners, slab, head_size) for b in (main, rest)], axis=1)
    summed = jnp.sum(lax.all_to_all(grams, ("place", "core"), 0, 0, tiled=True), axis=0)
    grams = lax.all_to_all(jnp.broadcast_to(summed[None], grams.shape), ("place", "core"), 0, 0, tiled=True)
    grams = grams.reshape(owners, 2, slab, head_size).transpose(1, 0, 2, 3)
    out_scale = update_gain * math.sqrt(max(row_count * owners, head_size))
    factors = poly_of_gram(grams.reshape(2, head_size, head_size), out_scale)
    update = split_product(main, factors[0])
    here = split_product(rest, factors[1])
    there = exchange(here, "side")
    cut = row_count - row_count // groups
    tail = jnp.broadcast_to(update[None, cut:], (groups, row_count - cut, head_size))
    tails = lax.all_to_all(tail, ("pair", "side"), 0, 0, tiled=True)
    updates = lax.all_gather(update[:cut], ("pair", "side"), axis=0)
    last = jnp.stack([jnp.where(side == 0, here, there), jnp.where(side == 0, there, here)])
    return jnp.concatenate([jnp.concatenate([updates, tails], axis=1), last], axis=0)


def solution(mesh):
    groups, owners = mesh.devices.shape
    split = Mesh(mesh.devices.reshape(groups // 2, 2, owners // 2, 2), ("pair", "side", "place", "core"))
    dp, fsdp = ("pair", "side"), ("place", "core")
    return jax.shard_map(
        local,
        mesh=split,
        in_specs=(P(dp, fsdp), P(dp, fsdp), P(dp + fsdp, None), P(dp + fsdp, None), P(None, fsdp, None), P(dp)),
        out_specs=P(None, fsdp, None),
        check_vma=False,
    )
```

```python
import math

import jax
import jax.numpy as jnp
from jax import lax
from jax.sharding import Mesh
from jax.sharding import PartitionSpec as P

ITERS = 3
EARLY = 32


coef_a = 3.4445
coef_b = -4.775
coef_c = 2.0315
momentum_decay = 0.95
update_gain = 0.2
norm_floor = 1e-07


def nesterov_blend(gradient, moment_rows):
    new_moment = momentum_decay * moment_rows + gradient
    return (gradient + momentum_decay * new_moment).astype(jnp.bfloat16)


def poly_of_gram(gram, out_scale):
    highest = lax.Precision.HIGHEST

    def mul(left, right):
        return jnp.einsum("mij,mjk->mik", left, right, precision=highest)

    size = gram.shape[-1]
    eye = jnp.eye(size, dtype=jnp.float32)[None]
    sum_squares = jnp.sum(gram * eye, axis=(1, 2), keepdims=True)
    inverse = 1.0 / (jnp.sqrt(sum_squares) + norm_floor)
    current = gram * inverse * inverse
    factor = eye * (inverse * out_scale)
    for iteration in range(ITERS):
        step = coef_a * eye + coef_b * current + coef_c * mul(current, current)
        factor = mul(factor, step) if iteration else factor[:, :1, :1] * step
        if iteration < ITERS - 1:
            current = mul(mul(current, step), step)
    return factor


def split_product(columns, factor):
    high = lax.reduce_precision(factor, 8, 7)
    contract = (((0,), (0,)), ((), ()))
    parts = [
        lax.dot_general(columns, part.astype(jnp.bfloat16), contract, preferred_element_type=jnp.float32)
        for part in (high, factor - high)
    ]
    return (parts[0] + parts[1]).astype(jnp.bfloat16)


def local(features, out_cotangent, head_cotangents, attention_out, momentum, lengths):
    tok_count, row_count = features.shape
    mat_count, _, head_size = momentum.shape
    own_tok = head_cotangents.shape[0]
    pairs, places = lax.axis_size("pair"), lax.axis_size("place")
    cores = lax.axis_size("core")
    groups, owners = 2 * pairs, places * cores
    in_mats = head_cotangents.shape[1] // head_size
    share = head_size // pairs
    late_width = head_size - EARLY
    pair, side, core = lax.axis_index("pair"), lax.axis_index("side"), lax.axis_index("core")

    def exchange(array, axis):
        return lax.ppermute(array, axis, [(0, 1), (1, 0)])

    def product(heads, rows):
        contract = (((0,), (0,)), ((), ()))
        return lax.dot_general(heads, rows, contract, preferred_element_type=jnp.float32)

    heads = jnp.concatenate([head_cotangents, attention_out], axis=1).reshape(own_tok, mat_count, head_size)
    late_heads = heads[:, :groups, EARLY:].reshape(own_tok, pairs, 2, late_width)
    late_heads = [late_heads[:, :, s].reshape(own_tok, pairs * late_width) for s in range(2)]
    late_heads = jnp.concatenate(
        [jnp.where(side == 0, late_heads[1], late_heads[0]), jnp.where(side == 0, late_heads[0], late_heads[1])],
        axis=1,
    )
    late_heads = lax.all_gather(late_heads, ("place", "core"), axis=0, tiled=True)

    early_own = jnp.concatenate(
        [
            heads[:, :groups, :EARLY].reshape(own_tok, groups * EARLY),
            heads[:, groups:].reshape(own_tok, (mat_count - groups) * head_size),
        ],
        axis=1,
    )
    mine = lax.all_to_all(
        jnp.broadcast_to(early_own[None], (places,) + early_own.shape), "place", 0, 0, tiled=True
    ).reshape(places * own_tok, early_own.shape[1])
    live_mask = (lax.iota(jnp.int32, tok_count) < lengths[0]).astype(jnp.bfloat16)[:, None]
    rows_in, rows_out = features * live_mask, out_cotangent * live_mask

    def halves(rows):
        split = rows.reshape(places, cores, own_tok, row_count)
        return [
            lax.dynamic_index_in_dim(split, which, 1, keepdims=False).reshape(-1, row_count)
            for which in (core, 1 - core)
        ]

    halves_in, halves_out = halves(rows_in), halves(rows_out)
    mine, halves_in, halves_out = lax.optimization_barrier((mine, halves_in, halves_out))
    other = exchange(mine, "core")
    cut = in_mats * EARLY
    early_in = product(mine[:, :cut], halves_in[0]) + product(other[:, :cut], halves_in[1])
    early_out = product(mine[:, cut:], halves_out[0]) + product(other[:, cut:], halves_out[1])
    early = jnp.concatenate([early_in, early_out], axis=0).astype(jnp.bfloat16)
    rest = early[groups * EARLY :].reshape(2, pairs, share, row_count).transpose(1, 0, 2, 3)
    early = jnp.concatenate(
        [early[: groups * EARLY].reshape(groups, EARLY, row_count), rest.reshape(groups, share, row_count)], axis=1
    )
    early = lax.all_to_all(early, ("pair", "side"), 0, 0, tiled=True)

    cut, whole = in_mats // 2 * late_width, pairs * late_width

    def late_part(at):
        part_in = product(late_heads[:, at : at + cut], features * live_mask)
        part_out = product(late_heads[:, at + cut : at + whole], out_cotangent * live_mask)
        return jnp.concatenate([part_in, part_out], axis=0)

    give, keep = late_part(0).astype(jnp.bfloat16), late_part(whole)
    early, give = lax.optimization_barrier((early, give))
    got = exchange(give, "side")
    late = (keep + got.astype(jnp.float32)).astype(jnp.bfloat16).reshape(pairs, late_width, row_count)
    early_sum = jnp.sum(early.astype(jnp.float32), axis=0)

    moment_main = lax.dynamic_index_in_dim(momentum, 2 * pair + side, 0, keepdims=False).T
    moment_rest = lax.dynamic_index_in_dim(momentum, groups + side, 0, keepdims=False).T
    moment_rest = lax.dynamic_slice_in_dim(moment_rest, pair * share, share, axis=0)
    rest = nesterov_blend(early_sum[EARLY:], moment_rest)

    late = jnp.concatenate([late, jnp.broadcast_to(rest[None], (pairs, share, row_count))], axis=1)
    late = lax.all_to_all(late, "pair", 0, 0, tiled=True)
    late_sum = jnp.sum(late[:, :late_width].astype(jnp.float32), axis=0)
    rest = late[:, late_width:].reshape(head_size, row_count)
    main = jnp.concatenate(
        [
            nesterov_blend(early_sum[:EARLY], moment_main[:EARLY]),
            nesterov_blend(late_sum, moment_main[EARLY:]),
        ],
        axis=0,
    )

    def gram(columns):
        return lax.dot_general(columns, columns, (((1,), (1,)), ((), ())), preferred_element_type=jnp.float32)

    slab = head_size // owners
    grams = jnp.concatenate([gram(b).reshape(owners, slab, head_size) for b in (main, rest)], axis=1)
    summed = jnp.sum(lax.all_to_all(grams, ("place", "core"), 0, 0, tiled=True), axis=0)
    grams = lax.all_to_all(jnp.broadcast_to(summed[None], grams.shape), ("place", "core"), 0, 0, tiled=True)
    grams = grams.reshape(owners, 2, slab, head_size).transpose(1, 0, 2, 3)
    out_scale = update_gain * math.sqrt(max(row_count * owners, head_size))
    factors = poly_of_gram(grams.reshape(2, head_size, head_size), out_scale)
    update = split_product(main, factors[0])
    here = split_product(rest, factors[1])
    there = exchange(here, "side")
    cut = row_count - row_count // groups
    tail = jnp.broadcast_to(update[None, cut:], (groups, row_count - cut, head_size))
    tails = lax.all_to_all(tail, ("pair", "side"), 0, 0, tiled=True)
    updates = lax.all_gather(update[:cut], ("pair", "side"), axis=0)
    last = jnp.stack([jnp.where(side == 0, here, there), jnp.where(side == 0, there, here)])
    last = lax.optimization_barrier(last)
    return jnp.concatenate([jnp.concatenate([updates, tails], axis=1), last], axis=0)


def solution(mesh):
    groups, owners = mesh.devices.shape
    split = Mesh(mesh.devices.reshape(groups // 2, 2, owners // 2, 2), ("pair", "side", "place", "core"))
    dp, fsdp = ("pair", "side"), ("place", "core")
    return jax.shard_map(
        local,
        mesh=split,
        in_specs=(P(dp, fsdp), P(dp, fsdp), P(dp + fsdp, None), P(dp + fsdp, None), P(None, fsdp, None), P(dp)),
        out_specs=P(None, fsdp, None),
        check_vma=False,
    )
```

```python
import math

import jax
import jax.numpy as jnp
from jax import lax
from jax.sharding import Mesh
from jax.sharding import PartitionSpec as P

ITERS = 3
EARLY = 32


coef_a = 3.4445
coef_b = -4.775
coef_c = 2.0315
momentum_decay = 0.95
update_gain = 0.2
norm_floor = 1e-07


def nesterov_blend(gradient, moment_rows):
    new_moment = momentum_decay * moment_rows + gradient
    return (gradient + momentum_decay * new_moment).astype(jnp.bfloat16)


def poly_of_gram(gram, out_scale):
    highest = lax.Precision.HIGHEST

    def mul(left, right):
        return jnp.einsum("mij,mjk->mik", left, right, precision=highest)

    size = gram.shape[-1]
    eye = jnp.eye(size, dtype=jnp.float32)[None]
    sum_squares = jnp.sum(gram * eye, axis=(1, 2), keepdims=True)
    inverse = 1.0 / (jnp.sqrt(sum_squares) + norm_floor)
    current = gram * inverse * inverse
    factor = eye * (inverse * out_scale)
    for iteration in range(ITERS):
        step = coef_a * eye + coef_b * current + coef_c * mul(current, current)
        factor = mul(factor, step) if iteration else factor[:, :1, :1] * step
        if iteration < ITERS - 1:
            current = mul(mul(current, step), step)
    return factor


def split_product(columns, factor):
    high = lax.reduce_precision(factor, 8, 7)
    contract = (((0,), (0,)), ((), ()))
    parts = [
        lax.dot_general(columns, part.astype(jnp.bfloat16), contract, preferred_element_type=jnp.float32)
        for part in (high, factor - high)
    ]
    return (parts[0] + parts[1]).astype(jnp.bfloat16)


def local(features, out_cotangent, head_cotangents, attention_out, momentum, lengths):
    tok_count, row_count = features.shape
    mat_count, _, head_size = momentum.shape
    own_tok = head_cotangents.shape[0]
    pairs, places = lax.axis_size("pair"), lax.axis_size("place")
    cores = lax.axis_size("core")
    groups, owners = 2 * pairs, places * cores
    in_mats = head_cotangents.shape[1] // head_size
    share = head_size // pairs
    late_width = head_size - EARLY
    pair, side, core = lax.axis_index("pair"), lax.axis_index("side"), lax.axis_index("core")

    def exchange(array, axis):
        return lax.ppermute(array, axis, [(0, 1), (1, 0)])

    def product(heads, rows):
        contract = (((0,), (0,)), ((), ()))
        return lax.dot_general(heads, rows, contract, preferred_element_type=jnp.float32)

    heads = jnp.concatenate([head_cotangents, attention_out], axis=1).reshape(own_tok, mat_count, head_size)
    late_heads = heads[:, :groups, EARLY:].reshape(own_tok, pairs, 2, late_width)
    late_heads = [late_heads[:, :, s].reshape(own_tok, pairs * late_width) for s in range(2)]
    late_heads = jnp.concatenate(
        [jnp.where(side == 0, late_heads[1], late_heads[0]), jnp.where(side == 0, late_heads[0], late_heads[1])],
        axis=1,
    )
    late_heads = lax.all_gather(late_heads, ("place", "core"), axis=0, tiled=True)

    early_own = jnp.concatenate(
        [
            heads[:, :groups, :EARLY].reshape(own_tok, groups * EARLY),
            heads[:, groups:].reshape(own_tok, (mat_count - groups) * head_size),
        ],
        axis=1,
    )
    mine = lax.all_to_all(
        jnp.broadcast_to(early_own[None], (places,) + early_own.shape), "place", 0, 0, tiled=True
    ).reshape(places * own_tok, early_own.shape[1])
    live_mask = (lax.iota(jnp.int32, tok_count) < lengths[0]).astype(jnp.bfloat16)[:, None]
    rows_in, rows_out = features * live_mask, out_cotangent * live_mask

    def halves(rows):
        split = rows.reshape(places, cores, own_tok, row_count)
        return [
            lax.dynamic_index_in_dim(split, which, 1, keepdims=False).reshape(-1, row_count)
            for which in (core, 1 - core)
        ]

    halves_in, halves_out = halves(rows_in), halves(rows_out)
    mine, halves_in, halves_out = lax.optimization_barrier((mine, halves_in, halves_out))
    other = exchange(mine, "core")
    cut = in_mats * EARLY
    early_in = product(mine[:, :cut], halves_in[0]) + product(other[:, :cut], halves_in[1])
    early_out = product(mine[:, cut:], halves_out[0]) + product(other[:, cut:], halves_out[1])
    early = jnp.concatenate([early_in, early_out], axis=0).astype(jnp.bfloat16)
    rest = early[groups * EARLY :].reshape(2, pairs, share, row_count).transpose(1, 0, 2, 3)
    early = jnp.concatenate(
        [early[: groups * EARLY].reshape(groups, EARLY, row_count), rest.reshape(groups, share, row_count)], axis=1
    )
    early = lax.all_to_all(early, ("pair", "side"), 0, 0, tiled=True)

    cut, whole = in_mats // 2 * late_width, pairs * late_width

    def late_part(at):
        part_in = product(late_heads[:, at : at + cut], features * live_mask)
        part_out = product(late_heads[:, at + cut : at + whole], out_cotangent * live_mask)
        return jnp.concatenate([part_in, part_out], axis=0)

    give, keep = late_part(0).astype(jnp.bfloat16), late_part(whole)
    early, keep = lax.optimization_barrier((early, keep))
    got = exchange(give, "side")
    late = (keep + got.astype(jnp.float32)).astype(jnp.bfloat16).reshape(pairs, late_width, row_count)
    early_sum = jnp.sum(early.astype(jnp.float32), axis=0)

    moment_main = lax.dynamic_index_in_dim(momentum, 2 * pair + side, 0, keepdims=False).T
    moment_rest = lax.dynamic_index_in_dim(momentum, groups + side, 0, keepdims=False).T
    moment_rest = lax.dynamic_slice_in_dim(moment_rest, pair * share, share, axis=0)
    rest = nesterov_blend(early_sum[EARLY:], moment_rest)

    late = jnp.concatenate([late, jnp.broadcast_to(rest[None], (pairs, share, row_count))], axis=1)
    late = lax.all_to_all(late, "pair", 0, 0, tiled=True)
    late_sum = jnp.sum(late[:, :late_width].astype(jnp.float32), axis=0)
    rest = late[:, late_width:].reshape(head_size, row_count)
    main = jnp.concatenate(
        [
            nesterov_blend(early_sum[:EARLY], moment_main[:EARLY]),
            nesterov_blend(late_sum, moment_main[EARLY:]),
        ],
        axis=0,
    )

    def gram(columns):
        return lax.dot_general(columns, columns, (((1,), (1,)), ((), ())), preferred_element_type=jnp.float32)

    slab = head_size // owners
    grams = jnp.concatenate([gram(b).reshape(owners, slab, head_size) for b in (main, rest)], axis=1)
    summed = jnp.sum(lax.all_to_all(grams, ("place", "core"), 0, 0, tiled=True), axis=0)
    grams = lax.all_to_all(jnp.broadcast_to(summed[None], grams.shape), ("place", "core"), 0, 0, tiled=True)
    grams = grams.reshape(owners, 2, slab, head_size).transpose(1, 0, 2, 3)
    out_scale = update_gain * math.sqrt(max(row_count * owners, head_size))
    factors = poly_of_gram(grams.reshape(2, head_size, head_size), out_scale)
    update = split_product(main, factors[0])
    here = split_product(rest, factors[1])
    there = exchange(here, "side")
    cut = row_count - row_count // groups
    tail = jnp.broadcast_to(update[None, cut:], (groups, row_count - cut, head_size))
    tails = lax.all_to_all(tail, ("pair", "side"), 0, 0, tiled=True)
    updates = lax.all_gather(update[:cut], ("pair", "side"), axis=0)
    last = jnp.stack([jnp.where(side == 0, here, there), jnp.where(side == 0, there, here)])
    last = lax.optimization_barrier(last)
    return jnp.concatenate([jnp.concatenate([updates, tails], axis=1), last], axis=0)


def solution(mesh):
    groups, owners = mesh.devices.shape
    split = Mesh(mesh.devices.reshape(groups // 2, 2, owners // 2, 2), ("pair", "side", "place", "core"))
    dp, fsdp = ("pair", "side"), ("place", "core")
    return jax.shard_map(
        local,
        mesh=split,
        in_specs=(P(dp, fsdp), P(dp, fsdp), P(dp + fsdp, None), P(dp + fsdp, None), P(None, fsdp, None), P(dp)),
        out_specs=P(None, fsdp, None),
        check_vma=False,
    )
```
